256 devices in a mesh: seq: 16 (over x, y), tp: 8 (over z), rep: 2 (over core).
Axes of the slice: x: 4, y: 4, z: 8, core: 2. Of those that a mesh axis runs over, the one named last changes fastest.
Arguments:
- prompt_x: bfloat16 [4, 8192, 16384], P('rep', 'seq', 'tp'), may hold values from -6 to 6
- prompt_bc: bfloat16 [4, 8192, 2, 8, 256], P('rep', 'seq', None, 'tp'), may hold values from -1.796875 to 1.796875
- prompt_dt: float32 [4, 8192, 256], P('rep', 'seq', 'tp'), may hold values from 0.3 to 3
- prompt_decay: float32 [4, 8192, 256], P('rep', 'seq', 'tp'), may hold values from -1.1 to 0
- lengths: int32 [4], P('rep'), may hold values from 256 to 8192, as said below
- owners: int32 [4], P('rep'), may hold values from 0 to 31, as said below
- gain: float32 [16384], P('tp'), may hold values from 0.5 to 1.5
- step_x: bfloat16 [32, 4, 16384], P(('seq', 'rep'), None, 'tp'), may hold values from -24 to 24
- step_bc: bfloat16 [32, 4, 2, 8, 256], P(('seq', 'rep'), None, None, 'tp'), may hold values from -1.796875 to 1.796875
- step_dt: float32 [32, 4, 256], P(('seq', 'rep'), None, 'tp'), may hold values from 0.3 to 3
- step_decay: float32 [32, 4, 256], P(('seq', 'rep'), None, 'tp'), may hold values from -0.7 to -0.02
Outputs:
- prefill_out: bfloat16 [4, 8192, 16384], P('rep', 'seq', 'tp')
- decode_out: bfloat16 [32, 4, 16384], P(('seq', 'rep'), None, 'tp')
The draws below stay inside these ranges and needn't reach their ends.
Inputs may be any that keep to these rules, and one draw needn't show every extreme that they name: `lengths`: every length is a multiple of 256, and in every draw some prompt has length 8192. `owners`: no two prompts share a slot, and slots 0, 15 and 31 are taken in every draw. Slot o stands for seq index o // 2 and rep index o % 2.
All inputs are finite; a program needn't handle non-finite values.
Results may differ from the reference program's by a relative error of at most 0.0055.
Values sent between devices are 32-bit elements; how exact they have to be, the bound alone decides.
No kernel may reach another device: no remote copies, remote signals or barrier semaphores. Data moves between devices by JAX's collectives and lax.ppermute only.
A program may use at most 192 MiB of HBM per device.

```python
import math
import jax
import jax.numpy as jnp
from jax import lax

STATE_HEADS = 256
N = 256
G = 8
STRETCH = 512
LEN_STEP = 256
TOK_DEV = 512
STEPS = 4
HP = 16384
PROMPT_LENGTH = 8192
PROMPT_COUNT = 4
SLOTS = 32


def draw_lengths(key, part):
    key = jax.random.fold_in(key, 11)
    first_key, second_key = jax.random.split(key)
    units_total = PROMPT_LENGTH // LEN_STEP
    drawn = jax.random.randint(first_key, (PROMPT_COUNT,), 1, units_total + 1) * LEN_STEP
    longest = jax.random.randint(second_key, (), 0, PROMPT_COUNT)
    return jnp.where(jnp.arange(PROMPT_COUNT) == longest, PROMPT_LENGTH, drawn).astype(jnp.int32)


def draw_owners(key, part):
    key = jax.random.fold_in(key, 12)
    first_key, second_key = jax.random.split(key)
    middle_slot = SLOTS // 2 - 1
    picked = jax.random.permutation(first_key, SLOTS - 3)[:PROMPT_COUNT - 3] + 1
    picked = jnp.where(picked >= middle_slot, picked + 1, picked)
    fixed_slots = jnp.array([0, middle_slot, SLOTS - 1], dtype=jnp.int32)
    ordered = jnp.concatenate([fixed_slots, picked.astype(jnp.int32)])
    placing = jax.random.permutation(second_key, PROMPT_COUNT)
    return ordered[placing].astype(jnp.int32)


def draw_prompt_decay(key, part):
    key = jax.random.fold_in(key, 13)
    random_keys = jax.random.split(key, 8)
    fast_share = 0.5
    region_count = PROMPT_LENGTH // TOK_DEV
    fast_heads = jax.random.uniform(random_keys[0], (STATE_HEADS,)) < fast_share
    region_fast = jax.random.uniform(random_keys[7], (PROMPT_COUNT, region_count, STATE_HEADS)) < 0.5
    region_fast = jnp.repeat(region_fast, TOK_DEV, axis=1)
    fast_here = jnp.logical_and(fast_heads[None, None, :], region_fast)
    fast_rate = jnp.exp(jax.random.uniform(random_keys[1], (STATE_HEADS,), minval=jnp.log(0.03), maxval=jnp.log(0.08)))
    slow_rate = jnp.exp(jax.random.uniform(random_keys[2], (STATE_HEADS,), minval=jnp.log(0.1), maxval=jnp.log(0.5))) / PROMPT_LENGTH
    baseline_rate = jnp.where(fast_here, fast_rate[None, None, :], slow_rate[None, None, :])
    jitter_level = jnp.exp(jax.random.uniform(random_keys[3], (PROMPT_COUNT, PROMPT_LENGTH, STATE_HEADS), minval=jnp.log(0.5), maxval=jnp.log(2.0)))
    regional_level = jnp.exp(jax.random.uniform(random_keys[4], (PROMPT_COUNT, region_count, STATE_HEADS), minval=jnp.log(0.5), maxval=jnp.log(2.0)))
    regional_level = jnp.repeat(regional_level, TOK_DEV, axis=1)
    spike_positions = jax.random.randint(random_keys[5], (PROMPT_COUNT, 3), 0, PROMPT_LENGTH)
    spike_flags = jnp.any(jnp.arange(PROMPT_LENGTH)[None, :, None] == spike_positions[:, None, :], axis=2)
    spike_depth = jax.random.uniform(random_keys[6], (PROMPT_COUNT, PROMPT_LENGTH, STATE_HEADS), minval=0.22, maxval=0.7)
    decay_factor = -(baseline_rate * jitter_level * regional_level) - jnp.where(spike_flags[:, :, None], spike_depth, 0.0)
    return decay_factor.astype(jnp.float32)


def steps_of(rng, dims, shards, least, largest):
    level, own = 1.0, jax.random.fold_in(rng, 6)
    for position, parts in shards:
        draws = jnp.exp(jax.random.uniform(jax.random.fold_in(own, position), (parts,), jnp.float32, least / len(shards), largest / len(shards)))
        level = level * jnp.repeat(draws, dims[position] // parts).reshape([-1 if axis == position else 1 for axis in range(len(dims))])
    return level


def gaussian(key, dims, deviation, reach, cuts=(), kind=jnp.bfloat16):
    level = steps_of(key, dims, cuts, -0.22, 0.18) if cuts else 1.0
    result = jax.random.normal(key, dims, jnp.float32) * deviation * level
    return jnp.minimum(jnp.maximum(result, -reach), reach).astype(kind)


def setup_inputs(seed: int = 0) -> dict:
    splits = jax.random.split(jax.random.key(seed), 12)
    return {
        "prompt_x": gaussian(splits[0], (PROMPT_COUNT, PROMPT_LENGTH, HP), 1.0, 6.0, ((0, 2), (1, 16), (2, 8))),
        "prompt_bc": gaussian(splits[1], (PROMPT_COUNT, PROMPT_LENGTH, 2, G, N), 0.3, 1.796875, ((0, 2), (1, 16), (3, 8))),
        "prompt_dt": jnp.clip(jnp.exp(math.log(3.0) - 2.3025851 * jax.random.uniform(splits[2], (PROMPT_COUNT, PROMPT_LENGTH, STATE_HEADS), jnp.float32) ** steps_of(splits[2], (PROMPT_COUNT, PROMPT_LENGTH, STATE_HEADS), ((0, 2), (1, 16), (2, 8)), -0.2, 0.2)), 0.3, 3.0),
        "prompt_decay": draw_prompt_decay(jax.random.fold_in(splits[11], 71), 0),
        "lengths": draw_lengths(jax.random.fold_in(splits[11], 71), 0),
        "owners": draw_owners(jax.random.fold_in(splits[11], 71), 0),
        "gain": jnp.clip(1.0 + 0.1 * jax.random.normal(splits[6], (HP,), jnp.float32), 0.5, 1.5),
        "step_x": gaussian(splits[7], (SLOTS, STEPS, HP), 4.0, 24.0, ((0, 32), (2, 8))),
        "step_bc": gaussian(splits[8], (SLOTS, STEPS, 2, G, N), 0.3, 1.796875, ((0, 32), (3, 8))),
        "step_dt": jnp.clip(jnp.exp(math.log(3.0) - 2.3025851 * jax.random.uniform(splits[9], (SLOTS, STEPS, STATE_HEADS), jnp.float32) ** steps_of(splits[9], (SLOTS, STEPS, STATE_HEADS), ((0, 32), (2, 8)), -0.2, 0.2)), 0.3, 3.0),
        "step_decay": jnp.clip(-0.7 + 0.68 * jax.random.uniform(splits[10], (SLOTS, STEPS, STATE_HEADS), jnp.float32) ** steps_of(splits[10], (SLOTS, STEPS, STATE_HEADS), ((0, 32), (2, 8)), -0.2, 0.2), -0.7, -0.02),
    }


eps_norm = 1e-05

def block_math(x_block, bc_block, rate_block, gate_block, before):
    row_count, block_len, heads = rate_block.shape
    groups = bc_block.shape[3]
    per_group = heads // groups
    head_size = x_block.shape[2] // heads
    highest = lax.Precision.HIGHEST
    running = jnp.cumsum(gate_block, axis=1)
    run_heads = jnp.swapaxes(running, 1, 2)
    key_rows = bc_block[:, :, 0].astype(jnp.float32)
    query_rows = bc_block[:, :, 1].astype(jnp.float32)
    scores = jnp.einsum('rtgn,rsgn->rgts', query_rows, key_rows, precision=highest)
    scores = jnp.repeat(scores, per_group, axis=1)
    causal = jnp.tril(jnp.ones((block_len, block_len), dtype=jnp.bool_))
    gap_matrix = jnp.where(causal, run_heads[:, :, :, None] - run_heads[:, :, None, :], -jnp.inf)
    mixing = (scores * jnp.exp(gap_matrix) * jnp.swapaxes(rate_block, 1, 2)[:, :, None, :]).astype(jnp.bfloat16)
    mixing = lax.optimization_barrier(mixing).astype(jnp.float32)
    values = x_block.reshape(row_count, block_len, heads, head_size).astype(jnp.float32)
    inner_term = jnp.einsum('rkts,rskp->rtkp', mixing, values, precision=highest)
    tail_weight = jnp.exp(running[:, -1:, :] - running) * rate_block
    weighted = (values * tail_weight[..., None]).astype(jnp.bfloat16)
    weighted = lax.optimization_barrier(weighted).astype(jnp.float32)
    weighted = weighted.reshape(row_count, block_len, groups, per_group, head_size)
    block_state = jnp.einsum('rsghp,rsgn->rghpn', weighted, key_rows, precision=highest)
    block_state = block_state.reshape(row_count, heads, head_size, -1)
    held_state = lax.optimization_barrier(before.astype(jnp.bfloat16)).astype(jnp.float32)
    held_state = held_state.reshape(row_count, groups, per_group, head_size, -1)
    outer_term = jnp.einsum('rtgn,rghpn->rtghp', query_rows, held_state, precision=highest)
    outer_term = outer_term.reshape(row_count, block_len, heads, head_size)
    mixed = inner_term + jnp.exp(running)[..., None] * outer_term
    return (mixed.reshape(row_count, block_len, heads * head_size), block_state, running[:, -1, :])

def reference(prompt_x, prompt_bc, prompt_dt, prompt_decay, lengths, owners, gain, step_x, step_bc, step_dt, step_decay):
    heads = prompt_dt.shape[2]
    groups = prompt_bc.shape[3]
    head_size = prompt_x.shape[2] // heads
    states_per_head = prompt_bc.shape[4]
    per_group = heads // groups
    highest = lax.Precision.HIGHEST
    positions = jnp.arange(PROMPT_LENGTH, dtype=jnp.int32)
    in_prompt = (positions[None, :] < lengths[:, None]).astype(jnp.float32)
    block_count = PROMPT_LENGTH // STRETCH

    def one_prompt(inputs):
        x_row, bc_row, rate_row, gate_row, mask_row = inputs
        gates = gate_row * mask_row[:, None]
        rates = rate_row * mask_row[:, None]

        def advance(carried, block_index):
            begin = (block_index * STRETCH).astype(jnp.int32)
            x_block = lax.dynamic_slice_in_dim(x_row, begin, STRETCH, 0)[None]
            bc_block = lax.dynamic_slice_in_dim(bc_row, begin, STRETCH, 0)[None]
            rate_block = lax.dynamic_slice_in_dim(rates, begin, STRETCH, 0)[None]
            gate_block = lax.dynamic_slice_in_dim(gates, begin, STRETCH, 0)[None]
            mixed, block_state, block_total = block_math(x_block, bc_block, rate_block, gate_block, carried[None])
            carried_next = jnp.exp(block_total[0])[:, None, None] * carried + block_state[0]
            return (carried_next, mixed[0])
        zero_state = jnp.zeros((heads, head_size, states_per_head), jnp.float32)
        final_state, mixed = lax.scan(advance, zero_state, jnp.arange(block_count, dtype=jnp.int32))
        mixed = mixed.reshape(PROMPT_LENGTH, heads * head_size) * mask_row[:, None]
        norms = lax.rsqrt(lax.optimization_barrier(jnp.mean(mixed * mixed, axis=1)) + eps_norm)
        return ((mixed * norms[:, None] * gain).astype(jnp.bfloat16), final_state)
    prefill_out, final_states = lax.map(one_prompt, (prompt_x, prompt_bc, prompt_dt, prompt_decay, in_prompt))
    slot_ids = jnp.arange(SLOTS, dtype=jnp.int32)
    choose = (owners[None, :] == slot_ids[:, None]).astype(jnp.float32)
    slot_states = jnp.einsum('op,pkxn->okxn', choose, final_states, precision=highest)
    filled = lax.optimization_barrier(jnp.sum(choose, axis=1))
    readings = []
    for step_index in range(STEPS):
        key_heads = jnp.repeat(step_bc[:, step_index, 0].astype(jnp.float32), per_group, axis=1)
        query_heads = jnp.repeat(step_bc[:, step_index, 1].astype(jnp.float32), per_group, axis=1)
        step_vals = step_x[:, step_index].astype(jnp.float32).reshape(SLOTS, heads, head_size)
        slot_states = jnp.exp(step_decay[:, step_index])[:, :, None, None] * slot_states + step_dt[:, step_index][:, :, None, None] * step_vals[:, :, :, None] * key_heads[:, :, None, :]
        reading = jnp.einsum('okxn,okn->okx', slot_states, query_heads, precision=highest)
        readings.append(reading.reshape(SLOTS, heads * head_size))
    readings = jnp.stack(readings, axis=1)
    norms = lax.rsqrt(lax.optimization_barrier(jnp.mean(readings * readings, axis=2)) + eps_norm)
    decode_out = (readings * norms[..., None] * gain * filled[:, None, None]).astype(jnp.bfloat16)
    return (prefill_out, decode_out)
```

```python
import functools

import jax
import jax.numpy as jnp
from jax import lax
from jax.experimental import pallas as pl
from jax.experimental.pallas import tpu as pltpu
from jax.sharding import PartitionSpec as P

eps_norm = 1e-05
TILE = 512
SUB = 128
HIGH = lax.Precision.HIGHEST
F32 = jnp.float32
BF16 = jnp.bfloat16


def remaining(lengths_ref, row, span):
    return lengths_ref[row] - lax.axis_index("seq") * span


def params(semantics, mib):
    return pltpu.CompilerParams(dimension_semantics=semantics, vmem_limit_bytes=mib * 2**20)


def split3(value):
    first = value.astype(BF16)
    rest = value - first.astype(F32)
    second = rest.astype(BF16)
    third = (rest - second.astype(F32)).astype(BF16)
    return jnp.concatenate([first, second, third], axis=0)


def head_columns(heads, head_size, start, width):
    row = lax.broadcasted_iota(jnp.int32, (3 * heads, width), 0)
    col = lax.broadcasted_iota(jnp.int32, (3 * heads, width), 1) + start
    return (lax.rem(row, heads) == col // head_size).astype(BF16)


def spread(parts, columns):
    return lax.dot_general(parts, columns, (((0,), (0,)), ((), ())), preferred_element_type=F32)


def prepare_kernel(lengths_ref, decay_ref, dt_ref, bc_ref, run_ref, tail_ref, end_ref, b_ref, c_ref):
    row = pl.program_id(0)
    heads, span = decay_ref.shape[1], decay_ref.shape[2]
    here = lax.broadcasted_iota(jnp.int32, (heads, span), 1) < remaining(lengths_ref, row, span)
    gates = jnp.where(here, decay_ref[0], 0.0)
    rates = jnp.where(here, dt_ref[0], 0.0)
    upto = (
        lax.broadcasted_iota(jnp.int32, (span, span), 0)
        <= lax.broadcasted_iota(jnp.int32, (span, span), 1)
    ).astype(BF16)
    sums = jnp.dot(split3(gates), upto, preferred_element_type=F32)
    running = sums[:heads] + sums[heads : 2 * heads] + sums[2 * heads :]
    run_ref[0] = running
    total = running[:, span - 1 : span]
    tail_ref[0] = split3(jnp.exp(total - running) * rates).T
    end_ref[0] = split3(jnp.broadcast_to(jnp.exp(total), (heads, SUB))).T[:16]
    b_ref[0] = bc_ref[0, :, 0, :].T
    c_ref[0] = bc_ref[0, :, 1, :]


def pre_kernel(head_size, owners_ref, tail_ref, end_ref, b_ref, query_ref, other_ref, x_ref, out_ref, keys_ref):
    tile, row = pl.program_id(0), pl.program_id(1)

    @pl.when(jnp.logical_and(tile == 0, row == 0))
    def _():
        chip = lax.axis_index("seq") * 2
        rep = lax.axis_index("rep")
        for prompt in range(2):
            mine = jnp.where(owners_ref[prompt] == chip + rep, 1.0, 0.0)
            other = jnp.where(owners_ref[prompt] == chip + 1 - rep, 1.0, 0.0)
            chosen = mine * query_ref[...] + other * other_ref[...]
            for half in range(2):
                keys_ref[8 * half + 4 * prompt : 8 * half + 4 * prompt + 4, :] = chosen[:, half * SUB : (half + 1) * SUB]

    heads, width, states = tail_ref.shape[2] // 3, x_ref.shape[2], b_ref.shape[1]
    columns = head_columns(heads, head_size, tile * width, width)
    weights = jnp.dot(tail_ref[row], columns, preferred_element_type=F32)
    weighted = (x_ref[0].astype(F32) * weights).astype(BF16)
    state = jnp.dot(b_ref[row], weighted, preferred_element_type=F32)
    ends = jnp.dot(end_ref[row], columns, preferred_element_type=F32)
    for chunk in range(out_ref.shape[0]):
        lanes = slice(chunk * SUB, (chunk + 1) * SUB)
        out_ref[chunk, pl.ds(pl.multiple_of(row * states, states), states), :] = state[:, lanes]
        out_ref[chunk, pl.ds(2 * states + row, 1), :] = ends[:1, lanes]

        @pl.when(row == 0)
        def _():
            out_ref[chunk, 2 * states + 8 :, :] = keys_ref[...]


def scan_kernel(in_ref, out_ref, carry_ref, key_ref, held_ref, sems):
    step = pl.program_id(0)
    count, states = in_ref.shape[0], 256

    @pl.when(step == 0)
    def _():
        carry_ref[...] = jnp.zeros_like(carry_ref)
        key_ref[...] = jnp.zeros_like(key_ref)

    for part in range(count):
        for row in range(2):
            rows = slice(row * states, (row + 1) * states)
            before = carry_ref[rows, :]
            held_ref[step * count + part, rows, :] = before
            carry_ref[rows, :] = (
                in_ref[part, 2 * states + row : 2 * states + row + 1, :] * before + in_ref[part, rows, :]
            )
        key_ref[...] += in_ref[part, 2 * states + 8 :, :]

    def send(k):
        parts = pl.ds(k * count, count)
        rows = pl.ds(0, 2 * states)
        return pltpu.make_async_copy(held_ref.at[parts, rows, :], out_ref.at[parts, rows, :], sems.at[k])

    send(step).start()

    @pl.when(step == pl.num_programs(0) - 1)
    def _():
        first, second = key_ref[:8, :], key_ref[8:, :]
        answers = []
        for row in range(2):
            upper = carry_ref[row * states : row * states + 128, :]
            lower = carry_ref[row * states + 128 : (row + 1) * states, :]
            answer = jnp.dot(first, upper, precision=HIGH, preferred_element_type=F32)
            answers.append(answer + jnp.dot(second, lower, precision=HIGH, preferred_element_type=F32))
        pick = lax.broadcasted_iota(jnp.int32, (8, 128), 0) < 4
        both = jnp.where(pick, answers[0], answers[1])
        total = held_ref.shape[0]
        for part in range(total):
            held_ref[part, 2 * states :, :] = both
        rest = pl.ds(2 * states, 8)
        last = pltpu.make_async_copy(held_ref.at[:, rest, :], out_ref.at[:, rest, :], sems.at[total // count])
        last.start()
        for k in range(total // count):
            send(k).wait()
        last.wait()


def inner_kernel(head_size, lengths_ref, run_ref, dt_ref, b_ref, c_ref, x_ref, out_ref, grow_ref, scores_ref, near_ref, mid_ref, far_ref, own_ref, other_ref):
    row, tile = pl.program_id(0), pl.program_id(1)
    heads, span = run_ref.shape[1], run_ref.shape[2]
    width = x_ref.shape[2]

    @pl.when(tile == 0)
    def _():
        running = run_ref[0]
        here = lax.broadcasted_iota(jnp.int32, (heads, span), 1) < remaining(lengths_ref, row, span)
        rates = jnp.where(here, dt_ref[0], 0.0)
        scores = jnp.dot(c_ref[0], b_ref[0], preferred_element_type=F32)
        causal = lax.broadcasted_iota(jnp.int32, (span, span), 0) >= lax.broadcasted_iota(
            jnp.int32, (span, span), 1
        )
        scores_ref[...] = jnp.where(causal, scores, 0.0).astype(BF16)

        def at(index):
            return running[:, index : index + 1]

        def blocks(references, start=0):
            return jnp.concatenate(
                [
                    jnp.broadcast_to(reference, (heads, SUB))
                    for reference in references
                ],
                axis=1,
            )

        middles = blocks([at(k * SUB + SUB // 2 - 1) for k in range(4)])
        near_ref[...] = split3(jnp.exp(middles - running) * rates)
        own_ref[...] = split3(jnp.where(here, jnp.exp(running - middles), 0.0))
        ends = blocks([at(SUB - 1), at(SUB - 1), at(3 * SUB - 1), at(3 * SUB - 1)])
        mid_ref[...] = split3(jnp.exp(jnp.minimum(ends - running, 0.0)) * rates)
        halves = jnp.broadcast_to(at(2 * SUB - 1), (heads, span))
        far_ref[...] = split3(jnp.exp(jnp.minimum(halves - running, 0.0)) * rates)
        starts = blocks([at(0), at(SUB - 1), at(2 * SUB - 1), at(3 * SUB - 1)])
        other_ref[...] = split3(jnp.where(here, jnp.exp(jnp.minimum(running - starts, 0.0)), 0.0))
        grow_ref[0] = split3(jnp.where(here, jnp.exp(running), 0.0)).T

    columns = head_columns(heads, head_size, tile * width, width)
    values = x_ref[0].astype(F32)

    def part(k, n=1):
        return slice(k * SUB, (k + n) * SUB)

    def weigh(parts, rows):
        return (values[rows] * spread(parts[:, rows], columns)).astype(BF16)

    def apply(rows, cols, weighted):
        return jnp.dot(scores_ref[rows, cols], weighted, preferred_element_type=F32)

    far = apply(part(2, 2), part(0, 2), weigh(far_ref, part(0, 2)))
    mids = [apply(part(1), part(0), weigh(mid_ref, part(0))), apply(part(3), part(2), weigh(mid_ref, part(2)))]
    running = run_ref[0]
    gap = jnp.exp(running[:, 3 * SUB - 1 : 3 * SUB] - running[:, 2 * SUB - 1 : 2 * SUB])
    gap = spread(split3(jnp.broadcast_to(gap, (heads, SUB))), columns)
    others = [None, mids[0], far[:SUB], mids[1] + gap * far[SUB:]]
    for k in range(4):
        near = apply(part(k), part(k), weigh(near_ref, part(k)))
        result = spread(own_ref[:, part(k)], columns) * near
        if others[k] is not None:
            result = result + spread(other_ref[:, part(k)], columns) * others[k]
        out_ref[0, part(k), :] = result.astype(BF16)


def post_kernel(head_size, grow_ref, c_ref, held_ref, inner_ref, out_ref, square_ref, total_ref):
    row, tile = pl.program_id(0), pl.program_id(1)
    heads = grow_ref.shape[2] // 3
    width = inner_ref.shape[2]

    @pl.when(tile == 0)
    def _():
        total_ref[...] = jnp.zeros_like(total_ref)

    columns = head_columns(heads, head_size, tile * width, width)
    held = jnp.concatenate([held_ref[k].astype(BF16) for k in range(held_ref.shape[0])], axis=1)
    outer = jnp.dot(c_ref[0], held, preferred_element_type=F32)
    grow = jnp.dot(grow_ref[0], columns, preferred_element_type=F32)
    mixed = inner_ref[0].astype(F32) + grow * outer
    out_ref[0] = mixed.astype(BF16)
    squares = mixed * mixed
    partial = total_ref[...]
    for k in range(width // SUB):
        partial += squares[:, k * SUB : (k + 1) * SUB]
    total_ref[...] = partial

    @pl.when(tile == pl.num_programs(1) - 1)
    def _():
        square_ref[0] = lax.dot_general(
            jnp.ones((8, SUB), F32),
            partial,
            (((1,), (1,)), ((), ())),
            precision=HIGH,
            preferred_element_type=F32,
        )


def decode_kernel(head_size, square_ref, mine_ref, own_ref, got_ref, factor_ref, x_ref, reading_ref, sums_ref):
    steps, width = x_ref.shape
    heads = factor_ref.shape[1]
    columns = head_columns(heads, head_size, 0, width)
    factors = spread(split3(factor_ref[...].T), columns)
    answers = own_ref[...]
    start = got_ref[:steps, :]
    for prompt in range(2):
        start = start + mine_ref[prompt] * answers[prompt * steps : (prompt + 1) * steps]
    values = x_ref[...].astype(F32)
    readings = factors[:steps] * start
    for j in range(steps):
        readings = readings + factors[(j + 1) * steps : (j + 2) * steps] * values[j : j + 1]
    reading_ref[...] = readings
    squares = jnp.broadcast_to(jnp.sum(readings * readings, axis=1, keepdims=True), (steps, SUB))
    blocks = square_ref.shape[2] // SUB
    for part in range(sums_ref.shape[0]):
        for row in range(2):
            for k in range(blocks):
                sums_ref[part, row * blocks + k : row * blocks + k + 1, :] = square_ref[row, :1, k * SUB : (k + 1) * SUB]
        sums_ref[part, 2 * blocks :, :] = squares


def final_kernel(channels, sums_ref, gain_ref, filled_ref, reading_ref, mixed_ref, out_ref, step_ref):
    row = pl.program_id(0)
    sums = jnp.sum(sums_ref[...], axis=0)
    scales = lax.rsqrt(sums / channels + eps_norm)
    gain = gain_ref[...]
    span = mixed_ref.shape[1]
    count = span // SUB
    mine = jnp.where(row == 0, scales[:count], scales[count : 2 * count])
    columns = jnp.concatenate([mine, mine], axis=0).T
    for k in range(count):
        rows = slice(k * SUB, (k + 1) * SUB)
        out_ref[0, rows, :] = (mixed_ref[0, rows, :].astype(F32) * columns[:, k : k + 1] * gain).astype(BF16)

    @pl.when(row == 0)
    def _():
        scale = scales[2 * count :, :1]
        step_ref[...] = (reading_ref[...] * scale * gain * filled_ref[0]).astype(BF16)


def local(prompt_x, prompt_bc, prompt_dt, prompt_decay, lengths, owners, gain, step_x, step_bc, step_dt, step_decay):
    rows, span, heads = prompt_dt.shape
    width = prompt_x.shape[2]
    head_size = width // heads
    states = prompt_bc.shape[4]
    steps = step_x.shape[1]
    channels = width * lax.axis_size("tp")
    seq_count = lax.axis_size("seq")
    seq_index, rep_index = lax.axis_index("seq"), lax.axis_index("rep")
    decay_t = jnp.swapaxes(prompt_decay, 1, 2)
    dt_t = jnp.swapaxes(prompt_dt, 1, 2)
    tiles = width // TILE
    per_tile = TILE // SUB
    smem = pl.BlockSpec(memory_space=pltpu.SMEM)

    my_slot = seq_index * 2 + rep_index
    other_slot = seq_index * 2 + 1 - rep_index
    queries = step_bc[0, :, 1, 0].astype(F32)
    swap = [(0, 1), (1, 0)]
    other_queries = lax.ppermute(queries, "rep", swap)
    mine = (owners == my_slot).astype(F32)
    other = (owners == other_slot).astype(F32)
    key_rows = 2 * rows * steps
    sent_rows = rows * states + 8 + key_rows
    bc = jnp.swapaxes(prompt_bc, 2, 3)[:, :, 0]
    per_row = lambda *dims: pl.BlockSpec((1,) + dims, lambda r: (r,) + (0,) * len(dims))
    whole = lambda *dims: pl.BlockSpec(dims, lambda *_: (0,) * len(dims))
    running, tails, ends, b_rows, c_rows = pl.pallas_call(
        prepare_kernel,
        grid=(rows,),
        in_specs=[smem, per_row(heads, span), per_row(heads, span), per_row(span, 2, states)],
        out_specs=[
            per_row(heads, span),
            per_row(span, 3 * heads),
            per_row(16, 3 * heads),
            per_row(states, span),
            per_row(span, states),
        ],
        out_shape=[
            jax.ShapeDtypeStruct((rows, heads, span), F32),
            jax.ShapeDtypeStruct((rows, span, 3 * heads), BF16),
            jax.ShapeDtypeStruct((rows, 16, 3 * heads), BF16),
            jax.ShapeDtypeStruct((rows, states, span), BF16),
            jax.ShapeDtypeStruct((rows, span, states), BF16),
        ],
        compiler_params=params(("arbitrary",), 60),
        name="prepare",
    )(lengths, decay_t, dt_t, bc)

    big = 1024
    sent = pl.pallas_call(
        functools.partial(pre_kernel, head_size),
        grid=(width // big, rows),
        in_specs=[
            smem,
            whole(rows, span, 3 * heads),
            whole(rows, 16, 3 * heads),
            whole(rows, states, span),
            whole(steps, states),
            whole(steps, states),
            pl.BlockSpec((1, span, big), lambda j, r: (r, 0, j)),
        ],
        out_specs=pl.BlockSpec((big // SUB, sent_rows, SUB), lambda j, r: (j, 0, 0)),
        out_shape=jax.ShapeDtypeStruct((width // SUB, sent_rows, SUB), F32),
        scratch_shapes=[pltpu.VMEM((key_rows, SUB), F32)],
        compiler_params=params(("arbitrary", "arbitrary"), 60),
        name="block_states",
    )(owners, tails, ends, b_rows, queries, other_queries, prompt_x)

    got = lax.all_to_all(sent, "seq", 0, 0)

    per_step = 4
    back_rows = rows * states + 8
    back = pl.pallas_call(
        scan_kernel,
        grid=(seq_count // per_step,),
        in_specs=[pl.BlockSpec((per_step, sent_rows, SUB), lambda k: (k, 0, 0))],
        out_specs=pl.BlockSpec(memory_space=pl.ANY),
        out_shape=jax.ShapeDtypeStruct((seq_count, back_rows, SUB), F32),
        scratch_shapes=[
            pltpu.VMEM((rows * states, SUB), F32),
            pltpu.VMEM((key_rows, SUB), F32),
            pltpu.VMEM((seq_count, back_rows, SUB), F32),
            pltpu.SemaphoreType.DMA((seq_count // per_step + 1,)),
        ],
        compiler_params=params(("arbitrary",), 60),
        name="prefix_states",
    )(got)

    held = lax.all_to_all(back, "seq", 0, 0)

    inner, grows = pl.pallas_call(
        functools.partial(inner_kernel, head_size),
        grid=(rows, tiles),
        in_specs=[
            smem,
            pl.BlockSpec((1, heads, span), lambda r, j: (r, 0, 0)),
            pl.BlockSpec((1, heads, span), lambda r, j: (r, 0, 0)),
            pl.BlockSpec((1, states, span), lambda r, j: (r, 0, 0)),
            pl.BlockSpec((1, span, states), lambda r, j: (r, 0, 0)),
            pl.BlockSpec((1, span, TILE), lambda r, j: (r, 0, j)),
        ],
        out_specs=[
            pl.BlockSpec((1, span, TILE), lambda r, j: (r, 0, j)),
            pl.BlockSpec((1, span, 3 * heads), lambda r, j: (r, 0, 0)),
        ],
        out_shape=[
            jax.ShapeDtypeStruct((rows, span, width), BF16),
            jax.ShapeDtypeStruct((rows, span, 3 * heads), BF16),
        ],
        scratch_shapes=[pltpu.VMEM((span, span), BF16)] + [pltpu.VMEM((3 * heads, span), BF16)] * 5,
        compiler_params=params(("arbitrary", "arbitrary"), 60),
        cost_estimate=pl.CostEstimate(flops=20 * 10**9, bytes_accessed=32 * 2**20, transcendentals=10**6),
        name="inner_terms",
    )(lengths, running, dt_t, b_rows, c_rows, prompt_x)

    answers = held[:, rows * states :, :].transpose(1, 0, 2).reshape(rows * steps, width)
    sent_answer = jnp.sum(other[:, None, None] * answers.reshape(rows, steps, width), axis=0)
    flags = jnp.broadcast_to(jnp.sum(other), (8 - steps, width))
    sent_answer, inner = lax.optimization_barrier((jnp.concatenate([sent_answer, flags], axis=0), inner))
    got_answer = lax.ppermute(sent_answer, "rep", swap)

    big = 1024
    mixed, squares = pl.pallas_call(
        functools.partial(post_kernel, head_size),
        grid=(rows, width // big),
        in_specs=[
            pl.BlockSpec((1, span, 3 * heads), lambda r, j: (r, 0, 0)),
            pl.BlockSpec((1, span, states), lambda r, j: (r, 0, 0)),
            pl.BlockSpec((big // SUB, states, SUB), lambda r, j: (j, r, 0)),
            pl.BlockSpec((1, span, big), lambda r, j: (r, 0, j)),
        ],
        out_specs=[
            pl.BlockSpec((1, span, big), lambda r, j: (r, 0, j)),
            pl.BlockSpec((1, 8, span), lambda r, j: (r, 0, 0)),
        ],
        out_shape=[
            jax.ShapeDtypeStruct((rows, span, width), BF16),
            jax.ShapeDtypeStruct((rows, 8, span), F32),
        ],
        scratch_shapes=[pltpu.VMEM((span, SUB), F32)],
        compiler_params=params(("arbitrary", "arbitrary"), 60),
        cost_estimate=pl.CostEstimate(flops=4 * 10**9, bytes_accessed=12 * 2**20, transcendentals=0),
        name="outer_terms",
    )(grows, c_rows, held, inner)

    keys_step = step_bc[0, :, 0, 0].astype(F32)
    sums = jnp.cumsum(step_decay[0], axis=0)
    products = jnp.einsum("jn,kn->jk", keys_step, queries, precision=HIGH)
    later = jnp.arange(steps)[:, None] <= jnp.arange(steps)[None, :]
    gaps = jnp.where(later[:, :, None], sums[None, :, :] - sums[:, None, :], -jnp.inf)
    factors = jnp.exp(gaps) * step_dt[0][:, None] * products[:, :, None]
    factors = jnp.concatenate([jnp.exp(sums)[None], factors], axis=0).reshape((steps + 1) * steps, heads)
    factors = jnp.pad(factors, ((0, 24 - factors.shape[0]), (0, 0)))
    tp_count = lax.axis_size("tp")
    readings, partial = pl.pallas_call(
        functools.partial(decode_kernel, head_size),
        in_specs=[
            pl.BlockSpec(memory_space=pltpu.VMEM),
            smem,
        ] + [pl.BlockSpec(memory_space=pltpu.VMEM)] * 4,
        out_shape=[
            jax.ShapeDtypeStruct((steps, width), F32),
            jax.ShapeDtypeStruct((tp_count, rows * span // SUB + steps, SUB), F32),
        ],
        name="decode",
    )(squares, mine, answers, got_answer, factors, step_x[0])
    filled = (jnp.sum(mine) + got_answer[steps, 0])
    gathered = lax.all_to_all(partial, "tp", 0, 0)
    prefill_out, decode_out = pl.pallas_call(
        functools.partial(final_kernel, float(channels)),
        grid=(rows, 2),
        in_specs=[
            whole(*gathered.shape),
            pl.BlockSpec((1, width // 2), lambda r, j: (0, j)),
            smem,
            pl.BlockSpec((steps, width // 2), lambda r, j: (0, j)),
            pl.BlockSpec((1, span, width // 2), lambda r, j: (r, 0, j)),
        ],
        out_specs=[
            pl.BlockSpec((1, span, width // 2), lambda r, j: (r, 0, j)),
            pl.BlockSpec((steps, width // 2), lambda r, j: (0, jnp.where(r == 0, j, 1))),
        ],
        out_shape=[
            jax.ShapeDtypeStruct((rows, span, width), BF16),
            jax.ShapeDtypeStruct((steps, width), BF16),
        ],
        compiler_params=params(("arbitrary", "arbitrary"), 60),
        name="normalize",
    )(gathered, gain[None], filled[None], readings, mixed)
    return (prefill_out, decode_out[None])


def solution(mesh):
    in_specs = (
        P("rep", "seq", "tp"),
        P("rep", "seq", None, "tp", None),
        P("rep", "seq", "tp"),
        P("rep", "seq", "tp"),
        P("rep"),
        P("rep"),
        P("tp"),
        P(("seq", "rep"), None, "tp"),
        P(("seq", "rep"), None, None, "tp", None),
        P(("seq", "rep"), None, "tp"),
        P(("seq", "rep"), None, "tp"),
    )
    out_specs = (P("rep", "seq", "tp"), P(("seq", "rep"), None, "tp"))
    return jax.shard_map(local, mesh=mesh, in_specs=in_specs, out_specs=out_specs, check_vma=False)
```

```python
import functools

import jax
import jax.numpy as jnp
from jax import lax
from jax.experimental import pallas as pl
from jax.experimental.pallas import tpu as pltpu
from jax.sharding import PartitionSpec as P

eps_norm = 1e-05
TILE = 512
SUB = 128
HIGH = lax.Precision.HIGHEST
F32 = jnp.float32
BF16 = jnp.bfloat16


def remaining(lengths_ref, row, span):
    return lengths_ref[row] - lax.axis_index("seq") * span


def params(semantics, mib):
    return pltpu.CompilerParams(dimension_semantics=semantics, vmem_limit_bytes=mib * 2**20)


def split3(value):
    first = value.astype(BF16)
    rest = value - first.astype(F32)
    second = rest.astype(BF16)
    third = (rest - second.astype(F32)).astype(BF16)
    return jnp.concatenate([first, second, third], axis=0)


def head_columns(heads, head_size, start, width):
    row = lax.broadcasted_iota(jnp.int32, (3 * heads, width), 0)
    col = lax.broadcasted_iota(jnp.int32, (3 * heads, width), 1) + start
    return (lax.rem(row, heads) == col // head_size).astype(BF16)


def spread(parts, columns):
    return lax.dot_general(parts, columns, (((0,), (0,)), ((), ())), preferred_element_type=F32)


def pre_kernel(head_size, lengths_ref, decay_in, dt_in, bc_in, x_in, out_hbm, run_ref, b_out_ref, out_ref, decay_ref, dt_ref, bc_ref, x_ref, tail_ref, end_ref, sems, x_sems, out_sems):
    rows, heads, span = decay_ref.shape
    width, states = x_ref.shape[2], bc_ref.shape[3]
    tile = width // 2

    def load(row):
        pairs = [(decay_in, decay_ref), (dt_in, dt_ref), (bc_in, bc_ref)]
        return [
            pltpu.make_async_copy(source.at[row], target.at[row], sems.at[row, k])
            for k, (source, target) in enumerate(pairs)
        ]

    def fetch(row, part):
        lanes = pl.ds(part * tile, tile)
        return pltpu.make_async_copy(x_in.at[row, :, lanes], x_ref.at[row, :, lanes], x_sems.at[row, part])

    def send(row, part):
        parts, inside = pl.ds(part * (tile // SUB), tile // SUB), pl.ds(row * states, states)
        return pltpu.make_async_copy(
            out_ref.at[parts, inside, :], out_hbm.at[parts, inside, :], out_sems.at[row, part]
        )

    def start(row):
        for copy in load(row):
            copy.start()
        for part in range(2):
            fetch(row, part).start()

    start(0)
    upto = (
        lax.broadcasted_iota(jnp.int32, (span, span), 0) <= lax.broadcasted_iota(jnp.int32, (span, span), 1)
    ).astype(BF16)
    for row in range(rows):
        for copy in load(row):
            copy.wait()
        here = lax.broadcasted_iota(jnp.int32, (heads, span), 1) < remaining(lengths_ref, row, span)
        gates = jnp.where(here, decay_ref[row], 0.0)
        rates = jnp.where(here, dt_ref[row], 0.0)
        sums = jnp.dot(split3(gates), upto, preferred_element_type=F32)
        running = sums[:heads] + sums[heads : 2 * heads] + sums[2 * heads :]
        run_ref[row] = running
        total = running[:, span - 1 : span]
        tail_ref[row] = split3(jnp.exp(total - running) * rates).T
        end_ref[row] = split3(jnp.broadcast_to(jnp.exp(total), (heads, SUB))).T[:16]
        b_out_ref[row] = bc_ref[row, :, 0, :].T
        if row + 1 < rows:
            start(row + 1)
        for part in range(2):
            columns = head_columns(heads, head_size, part * tile, tile)
            weights = jnp.dot(tail_ref[row], columns, preferred_element_type=F32)
            ends = jnp.dot(end_ref[row], columns, preferred_element_type=F32)
            fetch(row, part).wait()
            values = x_ref[row, :, part * tile : (part + 1) * tile].astype(F32)
            weighted = (values * weights).astype(BF16)
            state = jnp.dot(b_out_ref[row], weighted, preferred_element_type=F32)
            for k in range(tile // SUB):
                chunk, lanes = part * (tile // SUB) + k, slice(k * SUB, (k + 1) * SUB)
                out_ref[chunk, row * states : (row + 1) * states, :] = state[:, lanes]
                rest = slice(rows * states + 4 * row, rows * states + 4 * row + 4)
                out_ref[chunk, rest, :] = ends[:4, lanes]
            send(row, part).start()
    rest = pl.ds(rows * states, 8)
    last = pltpu.make_async_copy(out_ref.at[:, rest, :], out_hbm.at[:, rest, :], sems.at[0, 3])
    last.start()
    for row in range(rows):
        for part in range(2):
            send(row, part).wait()
    last.wait()


def keys_kernel(owners_ref, query_ref, other_ref, _, out_ref):
    half = pl.program_id(0)
    mine, other = slot_flags(owners_ref)
    chosen = [mine[p] * query_ref[...] + other[p] * other_ref[...] for p in range(2)]
    chosen = jnp.concatenate(chosen, axis=0)
    keys = jnp.where(half == 0, chosen[:, :SUB], chosen[:, SUB:])
    for chunk in range(out_ref.shape[0]):
        out_ref[chunk] = keys


def scan_kernel(in_ref, out_ref, carry_ref, key_ref, held_ref, sems):
    step = pl.program_id(0)
    count, states = in_ref.shape[0], 256

    @pl.when(step == 0)
    def _():
        carry_ref[...] = jnp.zeros_like(carry_ref)
        key_ref[...] = jnp.zeros_like(key_ref)

    for part in range(count):
        for row in range(2):
            rows = slice(row * states, (row + 1) * states)
            before = carry_ref[rows, :]
            held_ref[step * count + part, rows, :] = before
            carry_ref[rows, :] = (
                in_ref[part, 2 * states + 4 * row : 2 * states + 4 * row + 1, :] * before + in_ref[part, rows, :]
            )
        key_ref[...] += in_ref[part, 2 * states + 8 :, :]

    def send(k):
        parts = pl.ds(k * count, count)
        rows = pl.ds(0, 2 * states)
        return pltpu.make_async_copy(held_ref.at[parts, rows, :], out_ref.at[parts, rows, :], sems.at[k])

    send(step).start()

    @pl.when(step == pl.num_programs(0) - 1)
    def _():
        first, second = key_ref[:8, :], key_ref[8:, :]
        answers = []
        for row in range(2):
            upper = carry_ref[row * states : row * states + 128, :]
            lower = carry_ref[row * states + 128 : (row + 1) * states, :]
            answer = jnp.dot(first, upper, precision=HIGH, preferred_element_type=F32)
            answers.append(answer + jnp.dot(second, lower, precision=HIGH, preferred_element_type=F32))
        pick = lax.broadcasted_iota(jnp.int32, (8, 128), 0) < 4
        both = jnp.where(pick, answers[0], answers[1])
        total = held_ref.shape[0]
        for part in range(total):
            held_ref[part, 2 * states :, :] = both
        rest = pl.ds(2 * states, 8)
        last = pltpu.make_async_copy(held_ref.at[:, rest, :], out_ref.at[:, rest, :], sems.at[total // count])
        last.start()
        for k in range(total // count):
            send(k).wait()
        last.wait()


def inner_kernel(head_size, active, *refs):
    lengths_ref, run_in, dt_in, b_in, bc_in, x_in = refs[:6]
    refs = refs[6:] if active == 1 else refs[9:]
    out_ref, grow_out, c_out, run_ref, dt_ref, b_ref, bc_ref, x_buf, out_buf, grow_ref, c_ref = refs[:11]
    scores_ref, parts_ref, sems, in_sems, out_sems = refs[11:]
    rows, heads, span = run_ref.shape
    tiles = x_buf.shape[2] // TILE

    def fetch(row, tile):
        lanes = pl.ds(pl.multiple_of(tile * TILE, TILE), TILE)
        return pltpu.make_async_copy(x_in.at[row, :, lanes], x_buf.at[row, :, lanes], in_sems.at[row, tile])

    def send(row, tile):
        lanes = pl.ds(pl.multiple_of(tile * TILE, TILE), TILE)
        return pltpu.make_async_copy(out_buf.at[row, :, lanes], out_ref.at[row, :, lanes], out_sems.at[row, tile])

    def prepare(row):
        running = run_ref[row]
        here = lax.broadcasted_iota(jnp.int32, (heads, span), 1) < remaining(lengths_ref, row, span)
        rates = jnp.where(here, dt_ref[row], 0.0)
        c_ref[row] = bc_ref[row, :, 1, :]
        scores = jnp.dot(c_ref[row], b_ref[row], preferred_element_type=F32)
        causal = lax.broadcasted_iota(jnp.int32, (span, span), 0) >= lax.broadcasted_iota(
            jnp.int32, (span, span), 1
        )
        scores_ref[...] = jnp.where(causal, scores, 0.0).astype(BF16)

        def at(index):
            return running[:, index : index + 1]

        def blocks(references, start=0):
            return jnp.concatenate(
                [
                    jnp.broadcast_to(reference, (heads, SUB))
                    for reference in references
                ],
                axis=1,
            )

        middles = blocks([at(k * SUB + SUB // 2 - 1) for k in range(4)])
        near = jnp.exp(middles - running) * rates
        own = jnp.where(here, jnp.exp(running - middles), 0.0)
        ends = blocks([at(SUB - 1), at(3 * SUB - 1)])
        odd = jnp.concatenate([running[:, :SUB], running[:, 2 * SUB : 3 * SUB]], axis=1)
        odd_rates = jnp.concatenate([rates[:, :SUB], rates[:, 2 * SUB : 3 * SUB]], axis=1)
        mid = jnp.exp(ends - odd) * odd_rates
        halves = jnp.broadcast_to(at(2 * SUB - 1), (heads, 2 * SUB))
        far = jnp.exp(halves - running[:, : 2 * SUB]) * rates[:, : 2 * SUB]
        starts = blocks([at(SUB - 1), at(2 * SUB - 1), at(3 * SUB - 1)])
        other = jnp.where(here[:, SUB:], jnp.exp(running[:, SUB:] - starts), 0.0)
        gap = jnp.broadcast_to(jnp.exp(at(3 * SUB - 1) - at(2 * SUB - 1)), (heads, SUB))
        parts_ref[...] = split3(jnp.concatenate([near, own, mid, far, other, gap], axis=1)).T
        grow_ref[row] = split3(jnp.where(here, jnp.exp(running), 0.0)).T

    def one(row, tile):
        columns = head_columns(heads, head_size, tile * TILE, TILE)
        fetch(row, tile).wait()
        lanes = pl.ds(pl.multiple_of(tile * TILE, TILE), TILE)
        values = x_buf[row, :, lanes].astype(F32)

        wide = jnp.dot(parts_ref[...], columns, preferred_element_type=F32)
        near, own, mid, far, other, gap = (
            wide[low:high]
            for low, high in ((0, 512), (512, 1024), (1024, 1280), (1280, 1536), (1536, 1920), (1920, 1921))
        )

        def part(k, n=1):
            return slice(k * SUB, (k + n) * SUB)

        def apply(rows, cols, weights):
            weighted = (values[cols] * weights).astype(BF16)
            return jnp.dot(scores_ref[rows, cols], weighted, preferred_element_type=F32)

        far = apply(part(2, 2), part(0, 2), far)
        mids = [apply(part(1), part(0), mid[:SUB]), apply(part(3), part(2), mid[SUB:])]
        others = [None, mids[0], far[:SUB], mids[1] + gap * far[SUB:]]
        for k in range(4):
            result = own[part(k)] * apply(part(k), part(k), near[part(k)])
            if others[k] is not None:
                result = result + other[part(k - 1)] * others[k]
            out_buf[row, part(k), lanes] = result.astype(BF16)
        send(row, tile).start()

    @pl.when(lax.axis_index("rep") == active)
    def _():
        loads = [
            pltpu.make_async_copy(source, target, sems.at[k])
            for k, (source, target) in enumerate(
                [(run_in, run_ref), (dt_in, dt_ref), (b_in, b_ref), (bc_in, bc_ref)]
            )
        ]
        for load in loads:
            load.start()
        for row in range(rows):
            for tile in range(tiles):
                fetch(row, tile).start()
        for load in loads:
            load.wait()
        for row in range(rows):
            prepare(row)

            @pl.loop(0, tiles)
            def _(tile):
                one(row, tile)

        stores = [
            pltpu.make_async_copy(grow_ref, grow_out, sems.at[4]),
            pltpu.make_async_copy(c_ref, c_out, sems.at[5]),
        ]
        for store in stores:
            store.start()
        for row in range(rows):
            for tile in range(tiles):
                send(row, tile).wait()
        for store in stores:
            store.wait()


def post_kernel(head_size, grow_ref, c_ref, held_ref, inner_ref, out_ref, square_ref, total_ref):
    row, tile = pl.program_id(0), pl.program_id(1)
    heads = grow_ref.shape[2] // 3
    width = inner_ref.shape[2]

    @pl.when(tile == 0)
    def _():
        total_ref[...] = jnp.zeros_like(total_ref)

    columns = head_columns(heads, head_size, tile * width, width)
    held = jnp.concatenate([held_ref[k].astype(BF16) for k in range(held_ref.shape[0])], axis=1)
    outer = jnp.dot(c_ref[0], held, preferred_element_type=F32)
    grow = jnp.dot(grow_ref[0], columns, preferred_element_type=F32)
    mixed = inner_ref[0].astype(F32) + grow * outer
    out_ref[0] = mixed.astype(BF16)
    squares = mixed * mixed
    partial = total_ref[...]
    for k in range(width // SUB):
        partial += squares[:, k * SUB : (k + 1) * SUB]
    total_ref[...] = partial

    @pl.when(tile == pl.num_programs(1) - 1)
    def _():
        square_ref[0] = lax.dot_general(
            jnp.ones((8, SUB), F32),
            partial,
            (((1,), (1,)), ((), ())),
            precision=HIGH,
            preferred_element_type=F32,
        )


def slot_flags(owners_ref):
    chip, rep = lax.axis_index("seq") * 2, lax.axis_index("rep")
    mine = [jnp.where(owners_ref[prompt] == chip + rep, 1.0, 0.0) for prompt in range(2)]
    other = [jnp.where(owners_ref[prompt] == chip + 1 - rep, 1.0, 0.0) for prompt in range(2)]
    return mine, other


def answer_kernel(owners_ref, held_ref, own_ref, sent_ref):
    mine, other = slot_flags(owners_ref)
    steps = 4
    for ref, flags in ((own_ref, mine), (sent_ref, other)):
        for chunk in range(held_ref.shape[0]):
            lanes = slice(chunk * SUB, (chunk + 1) * SUB)
            ref[:steps, lanes] = flags[0] * held_ref[chunk, :steps] + flags[1] * held_ref[chunk, steps:]
        ref[steps:, :] = jnp.full((8 - steps, ref.shape[1]), flags[0] + flags[1], F32)


def decode_kernel(head_size, square_ref, own_ref, got_ref, x_ref, key_ref, query_ref, dt_ref, decay_ref, reading_ref, sums_ref):
    steps, width = x_ref.shape
    heads = dt_ref.shape[1]
    columns = head_columns(heads, head_size, 0, width)
    products = lax.dot_general(
        key_ref[...], query_ref[...], (((1,), (1,)), ((), ())), preferred_element_type=F32
    )
    factors, where = [], {}
    for k in range(steps):
        gone = jnp.zeros((1, heads), F32)
        for j in range(k, -1, -1):
            where[j, k] = len(factors)
            factors.append(jnp.exp(gone) * dt_ref[j : j + 1, :] * products[j : j + 1, k : k + 1])
            gone = gone + decay_ref[j : j + 1, :]
        where[-1, k] = len(factors)
        factors.append(jnp.exp(gone))
    while len(factors) % 8:
        factors.append(jnp.zeros((1, heads), F32))
    factors = spread(split3(jnp.concatenate(factors, axis=0).T), columns)
    start = own_ref[...] + got_ref[...]
    values = x_ref[...].astype(F32)
    readings = []
    for k in range(steps):
        reading = factors[where[-1, k] : where[-1, k] + 1] * start[k : k + 1]
        for j in range(k + 1):
            reading = reading + factors[where[j, k] : where[j, k] + 1] * values[j : j + 1]
        readings.append(reading)
    readings = jnp.concatenate(readings, axis=0)
    filled = start[steps : steps + 1]
    reading_ref[...] = readings * filled
    squares = jnp.broadcast_to(jnp.sum(readings * readings, axis=1, keepdims=True), (steps, SUB))
    blocks = square_ref.shape[2] // SUB
    for part in range(sums_ref.shape[0]):
        for row in range(2):
            for k in range(blocks):
                line = row * blocks + k
                sums_ref[part, line : line + 1, :] = square_ref[row, :1, k * SUB : (k + 1) * SUB]
        sums_ref[part, 2 * blocks :, :] = squares


def final_kernel(channels, sums_ref, gain_ref, reading_ref, mixed_ref, out_ref, step_ref):
    row = pl.program_id(0)
    sums = jnp.sum(sums_ref[...], axis=0)
    scales = lax.rsqrt(sums / channels + eps_norm)
    gain = gain_ref[...]
    count = mixed_ref.shape[1] // SUB
    mine = jnp.where(row == 0, scales[:count], scales[count : 2 * count])
    columns = jnp.concatenate([mine, mine], axis=0).T
    for k in range(count):
        rows = slice(k * SUB, (k + 1) * SUB)
        out_ref[0, rows, :] = (mixed_ref[0, rows, :].astype(F32) * columns[:, k : k + 1] * gain).astype(BF16)

    @pl.when(row == 0)
    def _():
        step_ref[...] = (reading_ref[...] * scales[2 * count :, :1] * gain).astype(BF16)


def after(value, *others):
    return lax.optimization_barrier((value,) + others)[0]


def local(prompt_x, prompt_bc, prompt_dt, prompt_decay, lengths, owners, gain, step_x, step_bc, step_dt, step_decay):
    rows, span, heads = prompt_dt.shape
    width = prompt_x.shape[2]
    head_size = width // heads
    states = prompt_bc.shape[4]
    steps = step_x.shape[1]
    channels = width * lax.axis_size("tp")
    seq_count = lax.axis_size("seq")
    decay_t = jnp.swapaxes(prompt_decay, 1, 2)
    dt_t = jnp.swapaxes(prompt_dt, 1, 2)
    smem = pl.BlockSpec(memory_space=pltpu.SMEM)

    queries = step_bc[0, :, 1, 0].astype(F32)
    swap = [(0, 1), (1, 0)]
    other_queries = lax.ppermute(queries, "rep", swap)
    key_rows = 2 * rows * steps
    sent_rows = rows * states + 8 + key_rows
    bc = jnp.swapaxes(prompt_bc, 2, 3)[:, :, 0]
    whole = lambda *dims: pl.BlockSpec(dims, lambda *_: (0,) * len(dims))
    anywhere = pl.BlockSpec(memory_space=pl.ANY)
    hbm = pl.BlockSpec(memory_space=pltpu.HBM)
    shape = jax.ShapeDtypeStruct

    vmem = pl.BlockSpec(memory_space=pltpu.VMEM)
    chunks = width // SUB
    sent, running, b_rows = pl.pallas_call(
        functools.partial(pre_kernel, head_size),
        in_specs=[smem] + [hbm] * 4,
        out_specs=[anywhere, vmem, vmem],
        out_shape=[
            shape((chunks, sent_rows, SUB), F32),
            shape((rows, heads, span), F32),
            shape((rows, states, span), BF16),
        ],
        scratch_shapes=[
            pltpu.VMEM((chunks, sent_rows, SUB), F32),
            pltpu.VMEM((rows, heads, span), F32),
            pltpu.VMEM((rows, heads, span), F32),
            pltpu.VMEM((rows, span, 2, states), BF16),
            pltpu.VMEM((rows, span, width), BF16),
            pltpu.VMEM((rows, span, 3 * heads), BF16),
            pltpu.VMEM((rows, 16, 3 * heads), BF16),
            pltpu.SemaphoreType.DMA((rows, 4)),
            pltpu.SemaphoreType.DMA((rows, 2)),
            pltpu.SemaphoreType.DMA((rows, 2)),
        ],
        compiler_params=params(None, 58),
        name="block_states",
    )(lengths, decay_t, dt_t, bc, prompt_x)

    def inner_terms(active, begin, results):
        return pl.pallas_call(
            functools.partial(inner_kernel, head_size, active),
            in_specs=[smem] + [anywhere] * 2 + [anywhere] + [hbm] * (2 + len(results)),
            out_specs=[hbm] * 3,
            out_shape=[
                shape((rows, span, width), BF16),
                shape((rows, span, 3 * heads), BF16),
                shape((rows, span, states), BF16),
            ],
            scratch_shapes=[
                pltpu.VMEM((rows, heads, span), F32),
                pltpu.VMEM((rows, heads, span), F32),
                pltpu.VMEM((rows, states, span), BF16),
                pltpu.VMEM((rows, span, 2, states), BF16),
                pltpu.VMEM((rows, span, width), BF16),
                pltpu.VMEM((rows, span, width), BF16),
                pltpu.VMEM((rows, span, 3 * heads), BF16),
                pltpu.VMEM((rows, span, states), BF16),
                pltpu.VMEM((span, span), BF16),
            ]
            + [
                pltpu.VMEM((4 * span, 3 * heads), BF16),
                pltpu.SemaphoreType.DMA((6,)),
                pltpu.SemaphoreType.DMA((rows, width // TILE)),
                pltpu.SemaphoreType.DMA((rows, width // TILE)),
            ],
            input_output_aliases={6 + k: k for k in range(len(results))},
            compiler_params=params(None, 58 if active else 28),
            name="inner_terms",
        )(begin, running, dt_t, b_rows, bc, prompt_x, *results)

    first = inner_terms(1, lengths, [])
    sent = pl.pallas_call(
        keys_kernel,
        grid=(2,),
        in_specs=[smem, whole(steps, states), whole(steps, states), anywhere],
        out_specs=pl.BlockSpec((chunks, 8, SUB), lambda k: (0, rows * states // 8 + 1 + k, 0)),
        out_shape=shape(sent.shape, F32),
        input_output_aliases={3: 0},
        compiler_params=params(("arbitrary",), 60),
        name="keys",
    )(owners, queries, other_queries, after(sent, *first))

    got = lax.all_to_all(sent, "seq", 0, 0)

    per_step = 8
    back_rows = rows * states + 8
    back = pl.pallas_call(
        scan_kernel,
        grid=(seq_count // per_step,),
        in_specs=[pl.BlockSpec((per_step, sent_rows, SUB), lambda k: (k, 0, 0))],
        out_specs=pl.BlockSpec(memory_space=pl.ANY),
        out_shape=jax.ShapeDtypeStruct((seq_count, back_rows, SUB), F32),
        scratch_shapes=[
            pltpu.VMEM((rows * states, SUB), F32),
            pltpu.VMEM((key_rows, SUB), F32),
            pltpu.VMEM((seq_count, back_rows, SUB), F32),
            pltpu.SemaphoreType.DMA((seq_count // per_step + 1,)),
        ],
        compiler_params=params(("arbitrary",), 16),
        name="prefix_states",
    )(got)

    held = lax.all_to_all(back, "seq", 0, 0)

    own_answer, sent_answer = pl.pallas_call(
        answer_kernel,
        grid=(1,),
        in_specs=[smem, pl.BlockSpec((chunks, 8, SUB), lambda k: (0, rows * states // 8, 0))],
        out_specs=[whole(8, width)] * 2,
        out_shape=[shape((8, width), F32)] * 2,
        compiler_params=params(("arbitrary",), 4),
        name="answers",
    )(owners, held)
    inner, grows, c_rows = inner_terms(0, after(lengths, sent_answer), first)
    got_answer = lax.ppermute(after(sent_answer, inner), "rep", swap)

    big = 1024
    mixed, squares = pl.pallas_call(
        functools.partial(post_kernel, head_size),
        grid=(rows, width // big),
        in_specs=[
            pl.BlockSpec((1, span, 3 * heads), lambda r, j: (r, 0, 0)),
            pl.BlockSpec((1, span, states), lambda r, j: (r, 0, 0)),
            pl.BlockSpec((big // SUB, states, SUB), lambda r, j: (j, r, 0)),
            pl.BlockSpec((1, span, big), lambda r, j: (r, 0, j)),
        ],
        out_specs=[
            pl.BlockSpec((1, span, big), lambda r, j: (r, 0, j)),
            pl.BlockSpec((1, 8, span), lambda r, j: (r, 0, 0)),
        ],
        out_shape=[
            shape((rows, span, width), BF16),
            shape((rows, 8, span), F32),
        ],
        scratch_shapes=[pltpu.VMEM((span, SUB), F32)],
        compiler_params=params(("arbitrary", "arbitrary"), 28),
        name="outer_terms",
    )(grows, c_rows, held, inner)

    tp_count = lax.axis_size("tp")
    readings, partial = pl.pallas_call(
        functools.partial(decode_kernel, head_size),
        in_specs=[vmem] * 8,
        out_shape=[shape((steps, width), F32), shape((tp_count, rows * span // SUB + steps, SUB), F32)],
        compiler_params=params(None, 8),
        name="decode",
    )(
        squares,
        own_answer,
        got_answer,
        step_x[0],
        step_bc[0, :, 0, 0],
        step_bc[0, :, 1, 0],
        step_dt[0],
        step_decay[0],
    )
    gathered = lax.all_to_all(partial, "tp", 0, 0)
    prefill_out, decode_out = pl.pallas_call(
        functools.partial(final_kernel, float(channels)),
        grid=(rows,),
        in_specs=[
            whole(*gathered.shape),
            whole(1, width),
            whole(steps, width),
            pl.BlockSpec((1, span, width), lambda r: (r, 0, 0)),
        ],
        out_specs=[pl.BlockSpec((1, span, width), lambda r: (r, 0, 0)), whole(steps, width)],
        out_shape=[shape((rows, span, width), BF16), shape((steps, width), BF16)],
        compiler_params=params(("arbitrary",), 20),
        name="normalize",
    )(gathered, gain[None], readings, mixed)
    return (prefill_out, decode_out[None])


def solution(mesh):
    in_specs = (
        P("rep", "seq", "tp"),
        P("rep", "seq", None, "tp", None),
        P("rep", "seq", "tp"),
        P("rep", "seq", "tp"),
        P("rep"),
        P("rep"),
        P("tp"),
        P(("seq", "rep"), None, "tp"),
        P(("seq", "rep"), None, None, "tp", None),
        P(("seq", "rep"), None, "tp"),
        P(("seq", "rep"), None, "tp"),
    )
    out_specs = (P("rep", "seq", "tp"), P(("seq", "rep"), None, "tp"))
    return jax.shard_map(local, mesh=mesh, in_specs=in_specs, out_specs=out_specs, check_vma=False)
```

```python
import functools

import jax
import jax.numpy as jnp
from jax import lax
from jax.experimental import pallas as pl
from jax.experimental.pallas import tpu as pltpu
from jax.sharding import PartitionSpec as P

eps_norm = 1e-05
EARLY, LATE = 512, 2048
SUB = 128
HIGH = lax.Precision.HIGHEST
F32 = jnp.float32
BF16 = jnp.bfloat16


def remaining(lengths_ref, row, span):
    return lengths_ref[row] - lax.axis_index("seq") * span


def params(semantics, mib):
    return pltpu.CompilerParams(dimension_semantics=semantics, vmem_limit_bytes=mib * 2**20)


def split3(value):
    first = value.astype(BF16)
    rest = value - first.astype(F32)
    second = rest.astype(BF16)
    third = (rest - second.astype(F32)).astype(BF16)
    return jnp.concatenate([first, second, third], axis=0)


def head_columns(heads, head_size, start, width):
    row = lax.broadcasted_iota(jnp.int32, (3 * heads, width), 0)
    col = lax.broadcasted_iota(jnp.int32, (3 * heads, width), 1) + start
    return (lax.rem(row, heads) == col // head_size).astype(BF16)


def spread(parts, columns):
    return lax.dot_general(parts, columns, (((0,), (0,)), ((), ())), preferred_element_type=F32)


def pre_kernel(head_size, lengths_ref, decay_in, dt_in, bc_in, x_in, out_hbm, run_ref, b_out_ref, out_ref, decay_ref, dt_ref, bc_ref, x_ref, tail_ref, end_ref, sems, x_sems, out_sems):
    rows, heads, span = decay_ref.shape
    width, states = x_ref.shape[2], bc_ref.shape[3]
    tile = width // 2

    def load(row):
        pairs = [(decay_in, decay_ref), (dt_in, dt_ref), (bc_in, bc_ref)]
        return [
            pltpu.make_async_copy(source.at[row], target.at[row], sems.at[row, k])
            for k, (source, target) in enumerate(pairs)
        ]

    def fetch(row, part):
        lanes = pl.ds(part * tile, tile)
        return pltpu.make_async_copy(x_in.at[row, :, lanes], x_ref.at[row, :, lanes], x_sems.at[row, part])

    def send(row, part):
        parts, inside = pl.ds(part * (tile // SUB), tile // SUB), pl.ds(row * states, states)
        return pltpu.make_async_copy(
            out_ref.at[parts, inside, :], out_hbm.at[parts, inside, :], out_sems.at[row, part]
        )

    def start(row):
        for copy in load(row):
            copy.start()
        for part in range(2):
            fetch(row, part).start()

    for row in range(rows):
        start(row)
    upto = (
        lax.broadcasted_iota(jnp.int32, (span, span), 0) <= lax.broadcasted_iota(jnp.int32, (span, span), 1)
    ).astype(BF16)
    for row in range(rows):
        for copy in load(row):
            copy.wait()
        here = lax.broadcasted_iota(jnp.int32, (heads, span), 1) < remaining(lengths_ref, row, span)
        gates = jnp.where(here, decay_ref[row], 0.0)
        rates = jnp.where(here, dt_ref[row], 0.0)
        sums = jnp.dot(split3(gates), upto, preferred_element_type=F32)
        running = sums[:heads] + sums[heads : 2 * heads] + sums[2 * heads :]
        run_ref[row] = running
        total = running[:, span - 1 : span]
        tail_ref[row] = split3(jnp.exp(total - running) * rates).T
        end_ref[row] = split3(jnp.broadcast_to(jnp.exp(total), (heads, SUB))).T[:16]
        b_out_ref[row] = bc_ref[row, :, 0, :].T
        for part in range(2):
            columns = head_columns(heads, head_size, part * tile, tile)
            weights = jnp.dot(tail_ref[row], columns, preferred_element_type=F32)
            ends = jnp.dot(end_ref[row], columns, preferred_element_type=F32)
            fetch(row, part).wait()
            values = x_ref[row, :, part * tile : (part + 1) * tile].astype(F32)
            weighted = (values * weights).astype(BF16)
            state = jnp.dot(b_out_ref[row], weighted, preferred_element_type=F32)
            for k in range(tile // SUB):
                chunk, lanes = part * (tile // SUB) + k, slice(k * SUB, (k + 1) * SUB)
                out_ref[chunk, row * states : (row + 1) * states, :] = state[:, lanes]
                rest = slice(rows * states + 4 * row, rows * states + 4 * row + 4)
                out_ref[chunk, rest, :] = ends[:4, lanes]
            send(row, part).start()
    rest = pl.ds(rows * states, 8)
    last = pltpu.make_async_copy(out_ref.at[:, rest, :], out_hbm.at[:, rest, :], sems.at[0, 3])
    last.start()
    for row in range(rows):
        for part in range(2):
            send(row, part).wait()
    last.wait()


def scan_kernel(in_ref, out_ref, carry_ref, key_ref, held_ref, sems):
    step = pl.program_id(0)
    count, states = in_ref.shape[0], 256

    @pl.when(step == 0)
    def _():
        carry_ref[...] = jnp.zeros_like(carry_ref)
        key_ref[...] = jnp.zeros_like(key_ref)

    for part in range(count):
        for row in range(2):
            rows = slice(row * states, (row + 1) * states)
            before = carry_ref[rows, :]
            held_ref[step * count + part, rows, :] = before
            carry_ref[rows, :] = (
                in_ref[part, 2 * states + 4 * row : 2 * states + 4 * row + 1, :] * before + in_ref[part, rows, :]
            )
        key_ref[...] += in_ref[part, 2 * states + 8 :, :]

    def send(k):
        parts = pl.ds(k * count, count)
        rows = pl.ds(0, 2 * states)
        return pltpu.make_async_copy(held_ref.at[parts, rows, :], out_ref.at[parts, rows, :], sems.at[k])

    send(step).start()

    @pl.when(step == pl.num_programs(0) - 1)
    def _():
        first, second = key_ref[:8, :], key_ref[8:, :]
        answers = []
        for row in range(2):
            upper = carry_ref[row * states : row * states + 128, :]
            lower = carry_ref[row * states + 128 : (row + 1) * states, :]
            answer = jnp.dot(first, upper, precision=HIGH, preferred_element_type=F32)
            answers.append(answer + jnp.dot(second, lower, precision=HIGH, preferred_element_type=F32))
        pick = lax.broadcasted_iota(jnp.int32, (8, 128), 0) < 4
        both = jnp.where(pick, answers[0], answers[1])
        total = held_ref.shape[0]
        for part in range(total):
            held_ref[part, 2 * states :, :] = both
        rest = pl.ds(2 * states, 8)
        last = pltpu.make_async_copy(held_ref.at[:, rest, :], out_ref.at[:, rest, :], sems.at[total // count])
        last.start()
        for k in range(total // count):
            send(k).wait()
        last.wait()


def inner_kernel(head_size, active, size, *refs):
    lengths_ref, run_in, dt_in, b_in, bc_in, x_in = refs[:6]
    if active == 1:
        owners_ref, query_ref, other_ref, _, out_ref, grow_out, c_out, sent_ref, keys_buf, keys_sem = refs[6:16]
        refs = refs[16:]
        mine, other = slot_flags(owners_ref)
        chosen = [mine[p] * query_ref[...] + other[p] * other_ref[...] for p in range(2)]
        chosen = jnp.concatenate(chosen, axis=0)
        for chunk in range(keys_buf.shape[0]):
            keys_buf[chunk, :8, :] = chosen[:, :SUB]
            keys_buf[chunk, 8:, :] = chosen[:, SUB:]
        count = keys_buf.shape[1]
        place = pl.ds(sent_ref.shape[1] - count, count)
        keys_copy = pltpu.make_async_copy(keys_buf, sent_ref.at[:, place, :], keys_sem)
        keys_copy.start()
    else:
        out_ref, grow_out, c_out = refs[9:12]
        refs = refs[12:]
    run_ref, dt_ref, b_ref, bc_ref, x_buf, out_buf, grow_ref, c_ref = refs[:8]
    scores_ref, parts_ref, sems, in_sems, out_sems = refs[8:]
    rows, heads, span = run_ref.shape
    tiles = x_buf.shape[2] // size

    def fetch(row, tile):
        lanes = pl.ds(pl.multiple_of(tile * size, size), size)
        return pltpu.make_async_copy(x_in.at[row, :, lanes], x_buf.at[row, :, lanes], in_sems.at[row, tile])

    def send(row, tile):
        lanes = pl.ds(pl.multiple_of(tile * size, size), size)
        return pltpu.make_async_copy(out_buf.at[row, :, lanes], out_ref.at[row, :, lanes], out_sems.at[row, tile])

    def prepare(row):
        running = run_ref[row]
        here = lax.broadcasted_iota(jnp.int32, (heads, span), 1) < remaining(lengths_ref, row, span)
        rates = jnp.where(here, dt_ref[row], 0.0)
        c_ref[row] = bc_ref[row, :, 1, :]
        scores = jnp.dot(c_ref[row], b_ref[row], preferred_element_type=F32)
        causal = lax.broadcasted_iota(jnp.int32, (span, span), 0) >= lax.broadcasted_iota(
            jnp.int32, (span, span), 1
        )
        scores_ref[...] = jnp.where(causal, scores, 0.0).astype(BF16)

        def at(index):
            return running[:, index : index + 1]

        def blocks(references, start=0):
            return jnp.concatenate(
                [
                    jnp.broadcast_to(reference, (heads, SUB))
                    for reference in references
                ],
                axis=1,
            )

        ends = [at((k + 1) * SUB - 1) for k in range(4)]
        halves = [at(k * SUB + SUB // 2 - 1) for k in range(4)]
        middles = blocks(halves)
        near = jnp.exp(middles - running) * rates
        own = jnp.where(here, jnp.exp(running - middles), 0.0)
        gaps = [
            ends[0] - halves[0],
            ends[2] - halves[2],
            ends[1] - halves[1],
            ends[1] - ends[0],
            ends[2] - ends[1],
            halves[1] - ends[0],
            halves[2] - ends[1],
            halves[3] - ends[2],
        ]
        gaps = jnp.exp(jnp.concatenate(gaps, axis=1))
        gaps = jnp.concatenate([gaps, jnp.zeros((heads, SUB - gaps.shape[1]), F32)], axis=1)
        parts_ref[...] = split3(jnp.concatenate([near, own, gaps], axis=1)).T
        grow_ref[row] = split3(jnp.where(here, jnp.exp(running), 0.0)).T

    def one(row, tile):
        columns = head_columns(heads, head_size, tile * size, size)
        fetch(row, tile).wait()
        lanes = pl.ds(pl.multiple_of(tile * size, size), size)
        values = x_buf[row, :, lanes].astype(F32)

        wide = jnp.dot(parts_ref[: 2 * span + 16], columns, preferred_element_type=F32)
        near, own = wide[:span], wide[span : 2 * span]
        gap = [wide[2 * span + k : 2 * span + k + 1] for k in range(8)]

        def part(k, n=1):
            return slice(k * SUB, (k + n) * SUB)

        def apply(rows, cols, weighted):
            return jnp.dot(scores_ref[rows, cols], weighted.astype(BF16), preferred_element_type=F32)

        weighted = values * near
        mids = [weighted[part(0)] * gap[0], weighted[part(2)] * gap[1]]
        far = jnp.concatenate([mids[0] * gap[3], weighted[part(1)] * gap[2]], axis=0)
        far = apply(part(2, 2), part(0, 2), far)
        mids = [apply(part(1), part(0), mids[0]), apply(part(3), part(2), mids[1])]
        others = [None, gap[5] * mids[0], gap[6] * far[:SUB], gap[7] * (mids[1] + gap[4] * far[SUB:])]
        for k in range(4):
            result = apply(part(k), part(k), weighted[part(k)])
            if others[k] is not None:
                result = result + others[k]
            out_buf[row, part(k), lanes] = (own[part(k)] * result).astype(BF16)
        send(row, tile).start()

    @pl.when(lax.axis_index("rep") == active)
    def _():
        loads = [
            pltpu.make_async_copy(source, target, sems.at[k])
            for k, (source, target) in enumerate(
                [(run_in, run_ref), (dt_in, dt_ref), (b_in, b_ref), (bc_in, bc_ref)]
            )
        ]
        for load in loads:
            load.start()
        for row in range(rows):
            for tile in range(tiles):
                fetch(row, tile).start()
        for load in loads:
            load.wait()
        for row in range(rows):
            prepare(row)

            @pl.loop(0, tiles)
            def _(tile):
                one(row, tile)

        stores = [
            pltpu.make_async_copy(grow_ref, grow_out, sems.at[4]),
            pltpu.make_async_copy(c_ref, c_out, sems.at[5]),
        ]
        for store in stores:
            store.start()
        for row in range(rows):
            for tile in range(tiles):
                send(row, tile).wait()
        for store in stores:
            store.wait()

    if active == 1:
        keys_copy.wait()


def post_kernel(head_size, grow_ref, c_ref, held_ref, inner_ref, out_ref, square_ref, total_ref):
    row, tile = pl.program_id(0), pl.program_id(1)
    heads = grow_ref.shape[2] // 3
    width = inner_ref.shape[2]

    @pl.when(tile == 0)
    def _():
        total_ref[...] = jnp.zeros_like(total_ref)

    columns = head_columns(heads, head_size, tile * width, width)
    held = jnp.concatenate([held_ref[k].astype(BF16) for k in range(held_ref.shape[0])], axis=1)
    outer = jnp.dot(c_ref[0], held, preferred_element_type=F32)
    grow = jnp.dot(grow_ref[0], columns, preferred_element_type=F32)
    mixed = inner_ref[0].astype(F32) + grow * outer
    out_ref[0] = mixed.astype(BF16)
    squares = mixed * mixed
    partial = total_ref[...]
    for k in range(width // SUB):
        partial += squares[:, k * SUB : (k + 1) * SUB]
    total_ref[...] = partial

    @pl.when(tile == pl.num_programs(1) - 1)
    def _():
        square_ref[0] = lax.dot_general(
            jnp.ones((8, SUB), F32),
            partial,
            (((1,), (1,)), ((), ())),
            precision=HIGH,
            preferred_element_type=F32,
        )


def slot_flags(owners_ref):
    chip, rep = lax.axis_index("seq") * 2, lax.axis_index("rep")
    mine = [jnp.where(owners_ref[prompt] == chip + rep, 1.0, 0.0) for prompt in range(2)]
    other = [jnp.where(owners_ref[prompt] == chip + 1 - rep, 1.0, 0.0) for prompt in range(2)]
    return mine, other


def answer_kernel(owners_ref, held_ref, own_ref, sent_ref):
    mine, other = slot_flags(owners_ref)
    steps = 4
    for ref, flags in ((own_ref, mine), (sent_ref, other)):
        for chunk in range(held_ref.shape[0]):
            lanes = slice(chunk * SUB, (chunk + 1) * SUB)
            ref[:steps, lanes] = flags[0] * held_ref[chunk, :steps] + flags[1] * held_ref[chunk, steps:]
        ref[steps:, :] = jnp.full((8 - steps, ref.shape[1]), flags[0] + flags[1], F32)


def decode_kernel(head_size, square_ref, own_ref, got_ref, x_ref, key_ref, query_ref, dt_ref, decay_ref, reading_ref, sums_ref):
    steps, width = x_ref.shape
    heads = dt_ref.shape[1]
    columns = head_columns(heads, head_size, 0, width)
    products = lax.dot_general(
        key_ref[...], query_ref[...], (((1,), (1,)), ((), ())), preferred_element_type=F32
    )
    factors, where = [], {}
    for k in range(steps):
        gone = jnp.zeros((1, heads), F32)
        for j in range(k, -1, -1):
            where[j, k] = len(factors)
            factors.append(jnp.exp(gone) * dt_ref[j : j + 1, :] * products[j : j + 1, k : k + 1])
            gone = gone + decay_ref[j : j + 1, :]
        where[-1, k] = len(factors)
        factors.append(jnp.exp(gone))
    while len(factors) % 8:
        factors.append(jnp.zeros((1, heads), F32))
    factors = spread(split3(jnp.concatenate(factors, axis=0).T), columns)
    start = own_ref[...] + got_ref[...]
    values = x_ref[...].astype(F32)
    readings = []
    for k in range(steps):
        reading = factors[where[-1, k] : where[-1, k] + 1] * start[k : k + 1]
        for j in range(k + 1):
            reading = reading + factors[where[j, k] : where[j, k] + 1] * values[j : j + 1]
        readings.append(reading)
    readings = jnp.concatenate(readings, axis=0)
    filled = start[steps : steps + 1]
    reading_ref[...] = readings * filled
    squares = jnp.broadcast_to(jnp.sum(readings * readings, axis=1, keepdims=True), (steps, SUB))
    blocks = square_ref.shape[2] // SUB
    for part in range(sums_ref.shape[0]):
        for row in range(2):
            for k in range(blocks):
                line = row * blocks + k
                sums_ref[part, line : line + 1, :] = square_ref[row, :1, k * SUB : (k + 1) * SUB]
        sums_ref[part, 2 * blocks :, :] = squares


def final_kernel(channels, sums_ref, gain_ref, reading_ref, mixed_ref, out_ref, step_ref):
    row = pl.program_id(0)
    sums = jnp.sum(sums_ref[...], axis=0)
    scales = lax.rsqrt(sums / channels + eps_norm)
    gain = gain_ref[...]
    count = mixed_ref.shape[1] // SUB
    mine = jnp.where(row == 0, scales[:count], scales[count : 2 * count])
    columns = jnp.concatenate([mine, mine], axis=0).T
    for k in range(count):
        rows = slice(k * SUB, (k + 1) * SUB)
        out_ref[0, rows, :] = (mixed_ref[0, rows, :].astype(F32) * columns[:, k : k + 1] * gain).astype(BF16)

    @pl.when(row == 0)
    def _():
        step_ref[...] = (reading_ref[...] * scales[2 * count :, :1] * gain).astype(BF16)


def total_over(value, axis):
    count, bit = lax.axis_size(axis), 1
    while bit < count:
        value = value + lax.ppermute(value, axis, [(k, k ^ bit) for k in range(count)])
        bit *= 2
    return value


def after(value, *others):
    return lax.optimization_barrier((value,) + others)[0]


def local(prompt_x, prompt_bc, prompt_dt, prompt_decay, lengths, owners, gain, step_x, step_bc, step_dt, step_decay):
    rows, span, heads = prompt_dt.shape
    width = prompt_x.shape[2]
    head_size = width // heads
    states = prompt_bc.shape[4]
    steps = step_x.shape[1]
    channels = width * lax.axis_size("tp")
    seq_count = lax.axis_size("seq")
    decay_t = jnp.swapaxes(prompt_decay, 1, 2)
    dt_t = jnp.swapaxes(prompt_dt, 1, 2)
    smem = pl.BlockSpec(memory_space=pltpu.SMEM)

    queries = step_bc[0, :, 1, 0].astype(F32)
    swap = [(0, 1), (1, 0)]
    other_queries = lax.ppermute(queries, "rep", swap)
    key_rows = 2 * rows * steps
    sent_rows = rows * states + 8 + key_rows
    bc = jnp.swapaxes(prompt_bc, 2, 3)[:, :, 0]
    whole = lambda *dims: pl.BlockSpec(dims, lambda *_: (0,) * len(dims))
    anywhere = pl.BlockSpec(memory_space=pl.ANY)
    shape = jax.ShapeDtypeStruct

    vmem = pl.BlockSpec(memory_space=pltpu.VMEM)
    chunks = width // SUB
    sent, running, b_rows = pl.pallas_call(
        functools.partial(pre_kernel, head_size),
        in_specs=[smem] + [anywhere] * 4,
        out_specs=[anywhere, vmem, vmem],
        out_shape=[
            shape((chunks, sent_rows, SUB), F32),
            shape((rows, heads, span), F32),
            shape((rows, states, span), BF16),
        ],
        scratch_shapes=[
            pltpu.VMEM((chunks, sent_rows, SUB), F32),
            pltpu.VMEM((rows, heads, span), F32),
            pltpu.VMEM((rows, heads, span), F32),
            pltpu.VMEM((rows, span, 2, states), BF16),
            pltpu.VMEM((rows, span, width), BF16),
            pltpu.VMEM((rows, span, 3 * heads), BF16),
            pltpu.VMEM((rows, 16, 3 * heads), BF16),
            pltpu.SemaphoreType.DMA((rows, 4)),
            pltpu.SemaphoreType.DMA((rows, 2)),
            pltpu.SemaphoreType.DMA((rows, 2)),
        ],
        compiler_params=params(None, 58),
        name="block_states",
    )(lengths, decay_t, dt_t, bc, prompt_x)

    def inner_terms(active, begin, more, results):
        early = active == 1
        size = EARLY if early else LATE
        return pl.pallas_call(
            functools.partial(inner_kernel, head_size, active, size),
            in_specs=[smem] + [anywhere] * 5 + ([smem, vmem, vmem, anywhere] if early else [anywhere] * 3),
            out_specs=[anywhere] * (4 if early else 3),
            out_shape=[
                shape((rows, span, width), BF16),
                shape((rows, span, 3 * heads), BF16),
                shape((rows, span, states), BF16),
            ]
            + [shape((chunks, sent_rows, SUB), F32)] * early,
            scratch_shapes=[pltpu.VMEM((chunks, key_rows, SUB), F32), pltpu.SemaphoreType.DMA] * early
            + [
                pltpu.VMEM((rows, heads, span), F32),
                pltpu.VMEM((rows, heads, span), F32),
                pltpu.VMEM((rows, states, span), BF16),
                pltpu.VMEM((rows, span, 2, states), BF16),
                pltpu.VMEM((rows, span, width), BF16),
                pltpu.VMEM((rows, span, width), BF16),
                pltpu.VMEM((rows, span, 3 * heads), BF16),
                pltpu.VMEM((rows, span, states), BF16),
                pltpu.VMEM((span, span), BF16),
                pltpu.VMEM((2 * span + SUB, 3 * heads), BF16),
                pltpu.SemaphoreType.DMA((6,)),
                pltpu.SemaphoreType.DMA((rows, width // size)),
                pltpu.SemaphoreType.DMA((rows, width // size)),
            ],
            input_output_aliases={9: 3} if early else {6 + k: k for k in range(3)},
            compiler_params=params(None, 58 if early else 40),
            name="inner_terms",
        )(begin, running, dt_t, b_rows, bc, prompt_x, *more, *results)

    *first, sent = inner_terms(1, lengths, [owners, queries, other_queries, sent], [])

    got = lax.all_to_all(sent, "seq", 0, 0)

    per_step = 8
    back_rows = rows * states + 8
    back = pl.pallas_call(
        scan_kernel,
        grid=(seq_count // per_step,),
        in_specs=[pl.BlockSpec((per_step, sent_rows, SUB), lambda k: (k, 0, 0))],
        out_specs=pl.BlockSpec(memory_space=pl.ANY),
        out_shape=jax.ShapeDtypeStruct((seq_count, back_rows, SUB), F32),
        scratch_shapes=[
            pltpu.VMEM((rows * states, SUB), F32),
            pltpu.VMEM((key_rows, SUB), F32),
            pltpu.VMEM((seq_count, back_rows, SUB), F32),
            pltpu.SemaphoreType.DMA((seq_count // per_step + 1,)),
        ],
        compiler_params=params(("arbitrary",), 16),
        name="prefix_states",
    )(got)

    held = lax.all_to_all(back, "seq", 0, 0)

    own_answer, sent_answer = pl.pallas_call(
        answer_kernel,
        grid=(1,),
        in_specs=[smem, pl.BlockSpec((chunks, 8, SUB), lambda k: (0, rows * states // 8, 0))],
        out_specs=[whole(8, width)] * 2,
        out_shape=[shape((8, width), F32)] * 2,
        compiler_params=params(("arbitrary",), 4),
        name="answers",
    )(owners, held)
    inner, grows, c_rows = inner_terms(0, after(lengths, sent_answer), [], first)
    got_answer = lax.ppermute(after(sent_answer, inner), "rep", swap)

    big = 1024
    mixed, squares = pl.pallas_call(
        functools.partial(post_kernel, head_size),
        grid=(rows, width // big),
        in_specs=[
            pl.BlockSpec((1, span, 3 * heads), lambda r, j: (r, 0, 0)),
            pl.BlockSpec((1, span, states), lambda r, j: (r, 0, 0)),
            pl.BlockSpec((big // SUB, states, SUB), lambda r, j: (j, r, 0)),
            pl.BlockSpec((1, span, big), lambda r, j: (r, 0, j)),
        ],
        out_specs=[
            pl.BlockSpec((1, span, big), lambda r, j: (r, 0, j)),
            pl.BlockSpec((1, 8, span), lambda r, j: (r, 0, 0)),
        ],
        out_shape=[
            shape((rows, span, width), BF16),
            shape((rows, 8, span), F32),
        ],
        scratch_shapes=[pltpu.VMEM((span, SUB), F32)],
        compiler_params=params(("arbitrary", "arbitrary"), 28),
        name="outer_terms",
    )(grows, c_rows, held, inner)

    readings, partial = pl.pallas_call(
        functools.partial(decode_kernel, head_size),
        in_specs=[vmem] * 8,
        out_shape=[shape((steps, width), F32), shape((1, rows * span // SUB + steps, SUB), F32)],
        compiler_params=params(None, 8),
        name="decode",
    )(
        squares,
        own_answer,
        got_answer,
        step_x[0],
        step_bc[0, :, 0, 0],
        step_bc[0, :, 1, 0],
        step_dt[0],
        step_decay[0],
    )
    gathered = total_over(partial, "tp")
    prefill_out, decode_out = pl.pallas_call(
        functools.partial(final_kernel, float(channels)),
        grid=(rows,),
        in_specs=[
            whole(*gathered.shape),
            whole(1, width),
            whole(steps, width),
            pl.BlockSpec((1, span, width), lambda r: (r, 0, 0)),
        ],
        out_specs=[pl.BlockSpec((1, span, width), lambda r: (r, 0, 0)), whole(steps, width)],
        out_shape=[shape((rows, span, width), BF16), shape((steps, width), BF16)],
        compiler_params=params(("arbitrary",), 20),
        name="normalize",
    )(gathered, gain[None], readings, mixed)
    return (prefill_out, decode_out[None])


def solution(mesh):
    in_specs = (
        P("rep", "seq", "tp"),
        P("rep", "seq", None, "tp", None),
        P("rep", "seq", "tp"),
        P("rep", "seq", "tp"),
        P("rep"),
        P("rep"),
        P("tp"),
        P(("seq", "rep"), None, "tp"),
        P(("seq", "rep"), None, None, "tp", None),
        P(("seq", "rep"), None, "tp"),
        P(("seq", "rep"), None, "tp"),
    )
    out_specs = (P("rep", "seq", "tp"), P(("seq", "rep"), None, "tp"))
    return jax.shard_map(local, mesh=mesh, in_specs=in_specs, out_specs=out_specs, check_vma=False)
```
